768 devices in a mesh: row: 128 (over y, z_lo, x), col: 6 (over z_hi, core).
Axes of the slice: x: 4, y: 8, z: 12 (z_hi: 3, z_lo: 4; z = z_hi * 4 + z_lo), core: 2. Of those that a mesh axis runs over, the one named last changes fastest.
Arguments:
- feats: bfloat16 [98304, 128], P(('col', 'row')), may hold values from -6 to 6
- weight: bfloat16 [128, 128], replicated, may hold values from -0.5 to 0.5
- tile_values: bfloat16 [128, 6, 96, 128, 128], P('row', 'col'), may hold values from -0.125 to 0.125
- tile_rows: int32 [128, 6, 96], P('row', 'col'), may hold values from 0 to 5
- tile_cols: int32 [128, 6, 96], P('row', 'col'), may hold values from 0 to 127
- relu_mask: int32 [98304, 128], P(('row', 'col')), may hold values from 0 to 1
- grad_out: bfloat16 [98304, 128], P(('row', 'col')), may hold values from -6 to 6
Outputs:
- preact: bfloat16 [98304, 128], P(('row', 'col'))
- grad_feats: float32 [98304, 128], P(('col', 'row'))
- grad_weight: float32 [128, 128], replicated
The draws below stay inside these ranges and needn't reach their ends.
Inputs may be any that keep to these rules, and one draw needn't show every extreme that they name: `tile_cols`: tiles may repeat a block; their entries then add.
All inputs are finite; a program needn't handle non-finite values.
Results may differ from the reference program's by a relative error of at most 0.0049.
Values may be sent and summed in bfloat16 or wider, within the bound.
No kernel may reach another device: no remote copies, remote signals or barrier semaphores. Data moves between devices by JAX's collectives and lax.ppermute only.
A program may use at most 64 MiB of HBM per device.

```python
import math
import jax
import jax.numpy as jnp
import numpy as np
from jax import lax

F = 128
BLK = 128
TILES = 96
RB = 6
GB = 128
NODES = 98304
N_ROW = 128
N_COL = 6


def place_ends(values, rng, smallest, largest):
    dims = values.shape
    place = [jax.random.randint(jax.random.fold_in(rng, axis), (), 0, dims[axis]) for axis in range(len(dims))]
    values = values.at[tuple(place)].set(smallest)
    longest = dims.index(max(dims))
    place[longest] = (place[longest] + 1) % dims[longest]
    return values.at[tuple(place)].set(largest)


def levels(key, dims, split, low, top_value):
    def one(dim, shards_of):
        steps = jax.random.uniform(jax.random.fold_in(jax.random.fold_in(key, 6), dim), (shards_of,), jnp.float32, low / len(split), top_value / len(split))
        return jnp.repeat(jnp.exp(steps), dims[dim] // shards_of).reshape((-1,) + (1,) * (len(dims) - dim - 1))

    level = one(*split[0])
    for cut in split[1:]:
        level = level * one(*cut)
    return level


def cumulative_ranks(count, skew):
    loads = [(1 << 20) // math.isqrt(standing ** skew) + 1 for standing in range(1, count + 1)]
    spread = 1 + sum(loads) // (1 << 30)
    return np.cumsum(np.array([max(1, weight // spread) for weight in loads]))


def ranked_ids(rng, extent, count, lean):
    grid = cumulative_ranks(count, lean)
    ticket = jax.random.randint(jax.random.fold_in(rng, 1), extent, 0, int(grid[count - 1]))
    rank = jnp.searchsorted(jnp.asarray(grid, jnp.int32), ticket, side="right")
    return jax.random.permutation(jax.random.fold_in(rng, 2), count)[rank].astype(jnp.int32)


def bell_draw(stream_key, dims, scale, reach, shards=(), kind=jnp.bfloat16):
    entries = jax.random.normal(stream_key, dims, jnp.float32) * scale
    if len(shards) > 0:
        entries = levels(stream_key, dims, shards, -0.22, 0.18) * entries
    return jnp.clip(entries, min=-reach, max=reach).astype(kind)


def setup_inputs(seed: int = 0) -> dict:
    seeds = jax.random.split(jax.random.key(seed), 8)
    feats = bell_draw(seeds[0], (NODES, F), 1.0, 6.0, ((0, 768),))
    weight = bell_draw(seeds[1], (F, F), F ** -0.5, 0.5)
    tile_values = bell_draw(seeds[2], (N_ROW, N_COL, TILES, BLK, BLK), (TILES * BLK // RB) ** -0.5, 0.125, ((0, 128), (1, 6)))
    tile_rows = place_ends(jax.random.randint(seeds[3], (N_ROW, N_COL, TILES), 0, RB), jax.random.fold_in(seeds[3], 1), 0, RB - 1).astype(jnp.int32)
    tile_cols = place_ends(ranked_ids(seeds[4], (N_ROW, N_COL, TILES), GB, 2), jax.random.fold_in(seeds[4], 3), 0, GB - 1).astype(jnp.int32)
    relu_mask = place_ends(jax.random.randint(seeds[5], (NODES, F), 0, 2), jax.random.fold_in(seeds[5], 1), 0, 1).astype(jnp.int32)
    grad_out = bell_draw(seeds[6], (NODES, F), 1.0, 6.0, ((0, 768),))
    return dict(feats=feats, weight=weight, tile_values=tile_values, tile_rows=tile_rows, tile_cols=tile_cols, relu_mask=relu_mask, grad_out=grad_out)


def reference(feats, weight, tile_values, tile_rows, tile_cols, relu_mask, grad_out):
    feat_blocks = feats.reshape(RB * N_ROW, BLK, F)
    row_ids = jnp.arange(RB, dtype=jnp.int32)

    def forward_row(index):
        tiles = tile_values[index].astype(jnp.float32)
        cols = index * 0 + tile_cols[index]
        global_cols = (jnp.arange(N_COL, dtype=jnp.int32)[:, None] * GB + cols).astype(jnp.int32)
        picked = feat_blocks[global_cols].astype(jnp.float32)
        prods = jnp.einsum('ckab,ckbf->ckaf', tiles, picked)
        onehot = (tile_rows[index][:, :, None] == row_ids[None, None, :]).astype(jnp.float32)
        summed = jnp.einsum('ckr,ckaf->raf', onehot, prods, precision=lax.Precision.HIGHEST)
        return summed.reshape(RB * BLK, F)
    agg = lax.map(forward_row, jnp.arange(N_ROW, dtype=jnp.int32)).reshape(NODES, F).astype(jnp.bfloat16)
    preact = jnp.dot(agg, weight, preferred_element_type=jnp.float32).astype(jnp.bfloat16)
    grad_pre = grad_out * relu_mask.astype(jnp.bfloat16)
    grad_agg = jnp.dot(grad_pre, weight.T, preferred_element_type=jnp.float32).astype(jnp.bfloat16)
    grad_blocks = grad_agg.reshape(RB * N_ROW, BLK, F)

    def backward_row(total, index):
        tiles = tile_values[index].astype(jnp.float32)
        global_rows = (index * RB + tile_rows[index]).astype(jnp.int32)
        picked = grad_blocks[global_rows].astype(jnp.float32)
        prods = jnp.einsum('ckba,ckbf->ckaf', tiles, picked)
        global_cols = (jnp.arange(N_COL, dtype=jnp.int32)[:, None] * GB + tile_cols[index]).astype(jnp.int32)
        total = total.at[global_cols.reshape(-1)].add(prods.reshape(N_COL * TILES, BLK, F))
        return (total, None)
    start = jnp.zeros((GB * N_COL, BLK, F), jnp.float32)
    grad_total, _ = lax.scan(backward_row, start, jnp.arange(N_ROW, dtype=jnp.int32))
    grad_feats = grad_total.reshape(NODES, F)
    grad_weight = jnp.dot(agg.T, grad_pre, preferred_element_type=jnp.float32) / jnp.sqrt(jnp.float32(NODES))
    return (preact, grad_feats, grad_weight)
```

```python
import math

import jax
import jax.numpy as jnp
from jax import lax
from jax.experimental import pallas as pl
from jax.experimental.pallas import tpu as pltpu
from jax.sharding import Mesh, PartitionSpec as P

SIZES = {"y": 8, "z": 4, "x": 4, "far": 3, "core": 2}
ROW = ("y", "z", "x")
COL = ("far", "core")
STEP = 4
VMEM = 48 * 1024 * 1024


def exchange(blocks, axes):
    return lax.all_to_all(blocks, axes, split_axis=0, concat_axis=0, tiled=True)


def spread(block, axes):
    count = math.prod(SIZES[axis] for axis in axes)
    return exchange(jnp.broadcast_to(block[None], (count,) + block.shape), axes)


def shift(block, by):
    count = SIZES["x"]
    return lax.ppermute(block, "x", [(i, (i + by) % count) for i in range(count)])


def add(*blocks):
    return sum(block.astype(jnp.float32) for block in blocks).astype(jnp.bfloat16)


def forward_kernel(rows_of, cols_of, values, panel, pre, after, out, local_weight, total):
    tiles = values.shape[0]
    total[...] = jnp.zeros_like(total)

    @pl.loop(0, tiles // STEP)
    def _(turn):
        at = [turn * STEP + i for i in range(STEP)]
        prods = [
            jnp.dot(values[k], panel[cols_of[k]], preferred_element_type=jnp.float32)
            for k in at
        ]
        for k, prod in zip(at, prods):
            total[rows_of[k]] += prod

    share = jnp.zeros(local_weight.shape, jnp.float32)
    for r in range(total.shape[0]):
        value = total[r]
        high = value.astype(jnp.bfloat16)
        low = (value - high.astype(jnp.float32)).astype(jnp.bfloat16)
        for part in (high, low):
            share += lax.dot_general(
                part, pre[r], (((0,), (0,)), ((), ())), preferred_element_type=jnp.float32
            )
        out[r] = value
    local_weight[...] = share


def backward_kernel(here, rows_of, cols_of, values, pre, weight, *refs):
    *outs, after, grads, total = refs
    tiles = values.shape[0]
    total[...] = jnp.zeros_like(total)
    for r in range(pre.shape[0]):
        grads[r] = lax.dot_general(
            weight[...], pre[r], (((1,), (1,)), ((), ())), preferred_element_type=jnp.float32
        ).astype(jnp.bfloat16)

    @pl.loop(0, tiles // STEP)
    def _(turn):
        at = [turn * STEP + i for i in range(STEP)]
        prods = [
            jnp.dot(grads[rows_of[k]], values[k], preferred_element_type=jnp.float32)
            for k in at
        ]
        for k, prod in zip(at, prods):
            total[cols_of[k]] += prod

    inner = SIZES["x"]
    half = outs[0].shape[0]

    @pl.loop(0, half)
    def _(j):
        for ahead in range(inner):
            x = lax.rem(here[0] + ahead, inner)
            for part in range(2):
                block = total[(part * half + j) * inner + x]
                outs[2 * ahead + part][j] = block.astype(jnp.bfloat16)

    after[...] = jnp.zeros_like(after)


def call(kernel, scalars, operands, out_shape, scratch, flops, moved):
    whole = pl.BlockSpec(memory_space=pltpu.VMEM)
    index = pl.BlockSpec(memory_space=pltpu.SMEM)
    return pl.pallas_call(
        kernel,
        out_shape=out_shape,
        in_specs=[index] * len(scalars) + [whole] * len(operands),
        out_specs=jax.tree.map(lambda _: whole, out_shape),
        scratch_shapes=scratch,
        compiler_params=pltpu.CompilerParams(vmem_limit_bytes=VMEM),
        cost_estimate=pl.CostEstimate(flops=flops, bytes_accessed=moved, transcendentals=0),
    )(*scalars, *operands)


def shards(feats, weight, tile_values, tile_rows, tile_cols, relu_mask, grad_out):
    values = tile_values[0, 0]
    rows_of = tile_rows[0, 0]
    cols_of = tile_cols[0, 0]
    tiles, block, _ = values.shape
    owned, width = feats.shape
    row_count = math.prod(SIZES[axis] for axis in COL)
    col_count = math.prod(SIZES[axis] for axis in ROW)
    flops = 2 * tiles * block * block * width

    with jax.named_scope("gather_near"):
        near = spread(feats, ("z", "x"))
    with jax.named_scope("gather_far"):
        panel = lax.all_gather(near.reshape(-1, width), "y", axis=0, tiled=True)
    panel = panel.reshape(col_count, block, width)

    grad_pre = grad_out * relu_mask.astype(jnp.bfloat16)
    with jax.named_scope("gather_grad"):
        pre = lax.all_gather(grad_pre, COL, axis=0, tiled=True).reshape(-1, block, width)

    here = lax.axis_index("x").astype(jnp.int32).reshape(1)
    half = col_count // SIZES["x"] // 2
    with jax.named_scope("backward"):
        *sums, after = call(
            backward_kernel, (here, rows_of, cols_of), (values, pre, weight),
            (jax.ShapeDtypeStruct((half, width, block), jnp.bfloat16),) * (2 * SIZES["x"])
            + (jax.ShapeDtypeStruct((8, 128), jnp.float32),),
            [
                pltpu.VMEM((row_count, width, block), jnp.bfloat16),
                pltpu.VMEM((col_count, width, block), jnp.float32),
            ],
            flops, 2 * values.size + 6 * col_count * block * width,
        )
    with jax.named_scope("scatter_x"):
        own, right, opposite, left = (sums[2 * i : 2 * i + 2] for i in range(SIZES["x"]))
        relay_right = shift(opposite[0], 1)
        relay_left = shift(opposite[1], -1)
        from_left_1 = shift(right[1], 1)
        from_right_0 = shift(left[0], -1)
        from_left_0 = shift(add(right[0], relay_right), 1)
        from_right_1 = shift(add(left[1], relay_left), -1)
        part = jnp.concatenate(
            [add(own[0], from_left_0, from_right_0), add(own[1], from_left_1, from_right_1)]
        )
    with jax.named_scope("scatter_yz"):
        got = exchange(part, ("y", "z"))
        grad_feats = jnp.sum(got.astype(jnp.float32), axis=0).T

    with jax.named_scope("forward"):
        partial_value, local_weight = call(
            forward_kernel, (rows_of, cols_of), (values, panel, pre, after),
            (
                jax.ShapeDtypeStruct((row_count, block, width), jnp.float32),
                jax.ShapeDtypeStruct((width, width), jnp.float32),
            ),
            [pltpu.VMEM((row_count, block, width), jnp.float32)],
            flops, 2 * values.size + 2 * panel.size,
        )
    with jax.named_scope("scatter_col"):
        agg = lax.psum_scatter(
            partial_value.reshape(-1, width), COL, scatter_dimension=0, tiled=True
        ).astype(jnp.bfloat16)
    preact = jnp.dot(agg, weight, preferred_element_type=jnp.float32).astype(jnp.bfloat16)

    with jax.named_scope("weight_sum"):
        near_axes, far_axes = ("z", "x", "core"), ("y", "far")
        pieces = math.prod(SIZES[axis] for axis in near_axes)
        piece = jnp.sum(exchange(local_weight.reshape(pieces, -1, width), near_axes), axis=0)
        piece = jnp.sum(spread(piece, far_axes), axis=0)
        grad_weight = spread(piece, near_axes).reshape(width, width)
    total_nodes = owned * row_count * col_count
    grad_weight = grad_weight / jnp.sqrt(jnp.float32(total_nodes))
    return (preact, grad_feats, grad_weight)


def solution(mesh):
    fine = Mesh(mesh.devices.reshape(tuple(SIZES.values())), tuple(SIZES))
    in_specs = (
        P(COL + ROW, None),
        P(),
        P(ROW, COL, None, None, None),
        P(ROW, COL, None),
        P(ROW, COL, None),
        P(ROW + COL, None),
        P(ROW + COL, None),
    )
    out_specs = (P(ROW + COL, None), P(COL + ROW, None), P())
    return jax.shard_map(shards, mesh=fine, in_specs=in_specs, out_specs=out_specs, check_vma=False)
```

```python
import math

import jax
import jax.numpy as jnp
from jax import lax
from jax.experimental import pallas as pl
from jax.experimental.pallas import tpu as pltpu
from jax.sharding import Mesh, PartitionSpec as P

SIZES = {"y": 8, "z": 4, "x": 4, "far": 3, "core": 2}
ROW = ("y", "z", "x")
COL = ("far", "core")
STEP = 4
CUTS = 2
VMEM = 48 * 1024 * 1024


def exchange(blocks, axes):
    return lax.all_to_all(blocks, axes, split_axis=0, concat_axis=0, tiled=True)


def spread(block, axes):
    count = math.prod(SIZES[axis] for axis in axes)
    return exchange(jnp.broadcast_to(block[None], (count,) + block.shape), axes)


def shift(block, axis, by):
    count = SIZES[axis]
    return lax.ppermute(block, axis, [(i, (i + by) % count) for i in range(count)])


def add(*blocks):
    return sum(block.astype(jnp.float32) for block in blocks).astype(jnp.bfloat16)


def col_block(here, ahead, other):
    far = lax.rem(here[1] + ahead, SIZES["far"])
    return far * SIZES["core"] + lax.rem(here[2] + other, SIZES["core"])


def forward_kernel(here, rows_of, cols_of, values, panel, *refs):
    *pres, after, own, others, local_weight, total = refs
    tiles = values.shape[0]
    total[...] = jnp.zeros_like(total)

    @pl.loop(0, tiles // STEP)
    def _(turn):
        at = [turn * STEP + i for i in range(STEP)]
        prods = [
            jnp.dot(values[k], panel[cols_of[k]], preferred_element_type=jnp.float32)
            for k in at
        ]
        for k, prod in zip(at, prods):
            total[rows_of[k]] += prod

    share = jnp.zeros(local_weight.shape, jnp.float32)
    for ahead, pre in enumerate(pres):
        for other, out in enumerate((own, others)):
            value = total[col_block(here, ahead, other)]
            high = value.astype(jnp.bfloat16)
            low = (value - high.astype(jnp.float32)).astype(jnp.bfloat16)
            for part in (high, low):
                share += lax.dot_general(
                    part, pre[other], (((0,), (0,)), ((), ())),
                    preferred_element_type=jnp.float32,
                )
            out[ahead] = value
    local_weight[...] = share


def backward_kernel(here, rows_of, cols_of, values, weight, *refs):
    pres, outs, (grads, total) = refs[: SIZES["far"]], refs[SIZES["far"] : -2], refs[-2:]
    tiles = values.shape[0]
    total[...] = jnp.zeros_like(total)
    for ahead, pre in enumerate(pres):
        for other in range(SIZES["core"]):
            grads[col_block(here, ahead, other)] = lax.dot_general(
                weight[...], pre[other], (((1,), (1,)), ((), ())),
                preferred_element_type=jnp.float32,
            ).astype(jnp.bfloat16)

    @pl.loop(0, tiles // STEP)
    def _(turn):
        at = [turn * STEP + i for i in range(STEP)]
        prods = [
            jnp.dot(grads[rows_of[k]], values[k], preferred_element_type=jnp.float32)
            for k in at
        ]
        for k, prod in zip(at, prods):
            total[cols_of[k]] += prod

    inner = SIZES["x"]
    half, rows, _ = outs[0].shape

    @pl.loop(0, half)
    def _(j):
        for ahead in range(inner):
            x = lax.rem(here[0] + ahead, inner)
            for part in range(2):
                block = (part * half + j) * inner + x
                for cut in range(CUTS):
                    out = outs[(cut * inner + ahead) * 2 + part]
                    out[j] = total[block, cut * rows : (cut + 1) * rows].astype(jnp.bfloat16)


def call(kernel, scalars, operands, out_shape, scratch, flops, moved):
    whole = pl.BlockSpec(memory_space=pltpu.VMEM)
    index = pl.BlockSpec(memory_space=pltpu.SMEM)
    return pl.pallas_call(
        kernel,
        out_shape=out_shape,
        in_specs=[index] * len(scalars) + [whole] * len(operands),
        out_specs=jax.tree.map(lambda _: whole, out_shape),
        scratch_shapes=scratch,
        compiler_params=pltpu.CompilerParams(vmem_limit_bytes=VMEM),
        cost_estimate=pl.CostEstimate(flops=flops, bytes_accessed=moved, transcendentals=0),
    )(*scalars, *operands)


def shards(feats, weight, tile_values, tile_rows, tile_cols, relu_mask, grad_out):
    values = tile_values[0, 0]
    rows_of = tile_rows[0, 0]
    cols_of = tile_cols[0, 0]
    tiles, block, _ = values.shape
    owned, width = feats.shape
    row_count = math.prod(SIZES[axis] for axis in COL)
    col_count = math.prod(SIZES[axis] for axis in ROW)
    flops = 2 * tiles * block * block * width
    here = jnp.stack([lax.axis_index(axis) for axis in ("x", "far", "core")]).astype(jnp.int32)

    grad_pre = grad_out * relu_mask.astype(jnp.bfloat16)
    with jax.named_scope("gather_grad"):
        pair = jnp.stack([grad_pre, shift(grad_pre, "core", 1)])
        feats, pair = lax.optimization_barrier((feats, pair))
        pres = (pair, shift(pair, "far", -1), shift(pair, "far", 1))

    with jax.named_scope("gather_near"):
        near = spread(feats, ("z", "x"))
    near, *pres = lax.optimization_barrier((near, *pres))
    with jax.named_scope("gather_far"):
        panel = lax.all_gather(near.reshape(-1, width), "y", axis=0, tiled=True)
    panel = panel.reshape(col_count, block, width)

    half, rows = col_count // SIZES["x"] // 2, width // CUTS
    with jax.named_scope("backward"):
        sums = call(
            backward_kernel, (here, rows_of, cols_of), (values, weight, *pres),
            (jax.ShapeDtypeStruct((half, rows, block), jnp.bfloat16),) * (2 * SIZES["x"] * CUTS),
            [
                pltpu.VMEM((row_count, width, block), jnp.bfloat16),
                pltpu.VMEM((col_count, width, block), jnp.float32),
            ],
            flops, 2 * values.size + 6 * col_count * block * width,
        )
    got = []
    relays = ()
    for cut in range(CUTS):
        each = sums[cut * 2 * SIZES["x"] : (cut + 1) * 2 * SIZES["x"]]
        each = lax.optimization_barrier((*each, *relays))[: len(each)]
        own, right, opposite, left = (each[2 * i : 2 * i + 2] for i in range(SIZES["x"]))
        with jax.named_scope("scatter_x"):
            relays = relay_right, relay_left = shift(opposite[0], "x", 1), shift(opposite[1], "x", -1)
            from_left_1 = shift(right[1], "x", 1)
            from_right_0 = shift(left[0], "x", -1)
            from_left_0 = shift(add(right[0], relay_right), "x", 1)
            from_right_1 = shift(add(left[1], relay_left), "x", -1)
            part = jnp.concatenate(
                [add(own[0], from_left_0, from_right_0), add(own[1], from_left_1, from_right_1)]
            )
        with jax.named_scope("scatter_yz"):
            got.append(exchange(part, ("y", "z")))

    with jax.named_scope("forward"):
        own, others, local_weight = call(
            forward_kernel, (here, rows_of, cols_of),
            (values, panel, *pres, got[0][0, :16] if CUTS > 1 else part[0, :16]),
            (
                jax.ShapeDtypeStruct((SIZES["far"], block, width), jnp.float32),
                jax.ShapeDtypeStruct((SIZES["far"], block, width), jnp.float32),
                jax.ShapeDtypeStruct((width, width), jnp.float32),
            ),
            [pltpu.VMEM((row_count, block, width), jnp.float32)],
            flops, 2 * values.size + 2 * panel.size,
        )
    with jax.named_scope("scatter_col"):
        mine = own + shift(others, "core", 1)

    local_weight, *got = lax.optimization_barrier((local_weight, *got))
    grad_feats = jnp.concatenate([jnp.sum(g.astype(jnp.float32), axis=0) for g in got]).T
    with jax.named_scope("weight_sum"):
        near_axes, far_axes = ("z", "x", "core"), ("y", "far")
        pieces = math.prod(SIZES[axis] for axis in near_axes)
        piece = jnp.sum(exchange(local_weight.reshape(pieces, -1, width), near_axes), axis=0)
        piece, mine = lax.optimization_barrier((piece, mine))
        away = shift(mine[1], "far", 1), shift(mine[2], "far", -1)
        piece = jnp.sum(spread(piece, far_axes), axis=0)
        piece, *away = lax.optimization_barrier((piece, *away))
        grad_weight = spread(piece, near_axes).reshape(width, width)
    agg = (mine[0] + away[0] + away[1]).astype(jnp.bfloat16)
    preact = jnp.dot(agg, weight, preferred_element_type=jnp.float32).astype(jnp.bfloat16)
    total_nodes = owned * row_count * col_count
    grad_weight = grad_weight / jnp.sqrt(jnp.float32(total_nodes))
    return (preact, grad_feats, grad_weight)


def solution(mesh):
    fine = Mesh(mesh.devices.reshape(tuple(SIZES.values())), tuple(SIZES))
    in_specs = (
        P(COL + ROW, None),
        P(),
        P(ROW, COL, None, None, None),
        P(ROW, COL, None),
        P(ROW, COL, None),
        P(ROW + COL, None),
        P(ROW + COL, None),
    )
    out_specs = (P(ROW + COL, None), P(COL + ROW, None), P())
    return jax.shard_map(shards, mesh=fine, in_specs=in_specs, out_specs=out_specs, check_vma=False)
```

```python
import math

import jax
import jax.numpy as jnp
from jax import lax
from jax.experimental import pallas as pl
from jax.experimental.pallas import tpu as pltpu
from jax.sharding import Mesh, PartitionSpec as P

SIZES = {"y": 8, "z": 4, "x": 4, "far": 3, "core": 2}
ROW = ("y", "z", "x")
COL = ("far", "core")
STEP = 4
VMEM = 48 * 1024 * 1024


def exchange(blocks, axes):
    return lax.all_to_all(blocks, axes, split_axis=0, concat_axis=0, tiled=True)


def spread(block, axes):
    count = math.prod(SIZES[axis] for axis in axes)
    return exchange(jnp.broadcast_to(block[None], (count,) + block.shape), axes)


def shift(block, axis, by):
    count = SIZES[axis]
    return lax.ppermute(block, axis, [(i, (i + by) % count) for i in range(count)])


def add(*blocks):
    return sum(block.astype(jnp.float32) for block in blocks).astype(jnp.bfloat16)


def col_block(here, ahead, other):
    far = lax.rem(here[1] + ahead, SIZES["far"])
    return far * SIZES["core"] + lax.rem(here[2] + other, SIZES["core"])


def forward_kernel(here, rows_of, cols_of, values, panel, *refs):
    pre, after, own, others, local_weight, total = refs
    tiles = values.shape[0]
    total[...] = jnp.zeros_like(total)

    @pl.loop(0, tiles // STEP)
    def _(turn):
        at = [turn * STEP + i for i in range(STEP)]
        prods = [
            jnp.dot(values[k], panel[cols_of[k]], preferred_element_type=jnp.float32)
            for k in at
        ]
        for k, prod in zip(at, prods):
            total[rows_of[k]] += prod

    share = jnp.zeros(local_weight.shape, jnp.float32)
    for r in range(total.shape[0]):
        value = total[r]
        high = value.astype(jnp.bfloat16)
        low = (value - high.astype(jnp.float32)).astype(jnp.bfloat16)
        for part in (high, low):
            share += lax.dot_general(
                part, pre[r], (((0,), (0,)), ((), ())), preferred_element_type=jnp.float32
            )
    for ahead in range(SIZES["far"]):
        for other, out in enumerate((own, others)):
            out[ahead] = total[col_block(here, ahead, other)]
    local_weight[...] = share


def backward_kernel(here, rows_of, cols_of, values, weight, pre, *refs):
    *outs, grads, total = refs
    tiles = values.shape[0]
    total[...] = jnp.zeros_like(total)
    for r in range(pre.shape[0]):
        grads[r] = lax.dot_general(
            weight[...], pre[r], (((1,), (1,)), ((), ())), preferred_element_type=jnp.float32
        ).astype(jnp.bfloat16)

    @pl.loop(0, tiles // STEP)
    def _(turn):
        at = [turn * STEP + i for i in range(STEP)]
        prods = [
            jnp.dot(grads[rows_of[k]], values[k], preferred_element_type=jnp.float32)
            for k in at
        ]
        for k, prod in zip(at, prods):
            total[cols_of[k]] += prod

    inner = SIZES["x"]
    half = outs[0].shape[0]

    @pl.loop(0, half)
    def _(j):
        for ahead in range(inner):
            x = lax.rem(here[0] + ahead, inner)
            for part in range(2):
                block = (part * half + j) * inner + x
                outs[2 * ahead + part][j] = total[block].astype(jnp.bfloat16)


def call(kernel, scalars, operands, out_shape, scratch, flops, moved):
    whole = pl.BlockSpec(memory_space=pltpu.VMEM)
    index = pl.BlockSpec(memory_space=pltpu.SMEM)
    return pl.pallas_call(
        kernel,
        out_shape=out_shape,
        in_specs=[index] * len(scalars) + [whole] * len(operands),
        out_specs=jax.tree.map(lambda _: whole, out_shape),
        scratch_shapes=scratch,
        compiler_params=pltpu.CompilerParams(vmem_limit_bytes=VMEM),
        cost_estimate=pl.CostEstimate(flops=flops, bytes_accessed=moved, transcendentals=0),
    )(*scalars, *operands)


def shards(feats, weight, tile_values, tile_rows, tile_cols, relu_mask, grad_out):
    values = tile_values[0, 0]
    rows_of = tile_rows[0, 0]
    cols_of = tile_cols[0, 0]
    tiles, block, _ = values.shape
    owned, width = feats.shape
    row_count = math.prod(SIZES[axis] for axis in COL)
    col_count = math.prod(SIZES[axis] for axis in ROW)
    flops = 2 * tiles * block * block * width
    here = jnp.stack([lax.axis_index(axis) for axis in ("x", "far", "core")]).astype(jnp.int32)

    grad_pre = grad_out * relu_mask.astype(jnp.bfloat16)
    with jax.named_scope("gather_near"):
        near = spread(feats, ("z", "x"))
    with jax.named_scope("gather_grad"):
        pre = lax.all_gather(grad_pre, COL, axis=0, tiled=True).reshape(-1, block, width)
    near, pre = lax.optimization_barrier((near, pre))
    with jax.named_scope("gather_far"):
        panel = lax.all_gather(near.reshape(-1, width), "y", axis=0, tiled=True)
    panel = panel.reshape(col_count, block, width)

    half = col_count // SIZES["x"] // 2
    with jax.named_scope("backward"):
        sums = call(
            backward_kernel, (here, rows_of, cols_of), (values, weight, pre),
            (jax.ShapeDtypeStruct((half, width, block), jnp.bfloat16),) * (2 * SIZES["x"]),
            [
                pltpu.VMEM((row_count, width, block), jnp.bfloat16),
                pltpu.VMEM((col_count, width, block), jnp.float32),
            ],
            flops, 2 * values.size + 6 * col_count * block * width,
        )
    own, right, opposite, left = (sums[2 * i : 2 * i + 2] for i in range(SIZES["x"]))
    with jax.named_scope("scatter_x"):
        relay_right = shift(opposite[0], "x", 1)
        relay_left = shift(opposite[1], "x", -1)
        from_left_1 = shift(right[1], "x", 1)
        from_right_0 = shift(left[0], "x", -1)
        from_left_0 = shift(add(right[0], relay_right), "x", 1)
        from_right_1 = shift(add(left[1], relay_left), "x", -1)
        part = (
            add(own[0], from_left_0, from_right_0), add(own[1], from_left_1, from_right_1)
        )

    with jax.named_scope("forward"):
        own_sums, other_sums, local_weight = call(
            forward_kernel, (here, rows_of, cols_of),
            (values, panel, pre, part[0][0, :16] + part[1][0, :16]),
            (
                jax.ShapeDtypeStruct((SIZES["far"], block, width), jnp.float32),
                jax.ShapeDtypeStruct((SIZES["far"], block, width), jnp.float32),
                jax.ShapeDtypeStruct((width, width), jnp.float32),
            ),
            [pltpu.VMEM((row_count, block, width), jnp.float32)],
            flops, 2 * values.size + 2 * panel.size,
        )
    with jax.named_scope("scatter_yz"):
        pieces = SIZES["y"] * SIZES["z"]
        rest, parts = local_weight.reshape(pieces, -1, width), []
        for _ in range(3):
            parts.append(rest.astype(jnp.bfloat16))
            rest = rest - parts[-1].astype(jnp.float32)
        lines = parts[0].shape[1]
        pad = jnp.zeros((pieces, 4 * lines - 3 * lines, width), jnp.bfloat16)
        riders = jnp.concatenate(parts + [pad], axis=1)
        got = exchange(
            jnp.concatenate([jnp.concatenate(part), riders], axis=1), ("y", "z")
        )
    with jax.named_scope("scatter_col"):
        mine = own_sums + shift(other_sums, "core", 1)
        away = shift(mine[1], "far", 1), shift(mine[2], "far", -1)
    got, *away = lax.optimization_barrier((got, *away))
    got = jnp.sum(got.astype(jnp.float32), axis=0)
    grad_feats = got[:width].T
    with jax.named_scope("weight_sum"):
        piece = got[width : width + 3 * lines].reshape(3, lines, width).sum(axis=0)
        piece = jnp.sum(spread(piece, ("x", "far", "core")), axis=0)
        grad_weight = spread(piece, ("y", "z")).reshape(width, width)
    agg = (mine[0] + away[0] + away[1]).astype(jnp.bfloat16)
    preact = jnp.dot(agg, weight, preferred_element_type=jnp.float32).astype(jnp.bfloat16)
    total_nodes = owned * row_count * col_count
    grad_weight = grad_weight / jnp.sqrt(jnp.float32(total_nodes))
    return (preact, grad_feats, grad_weight)


def solution(mesh):
    fine = Mesh(mesh.devices.reshape(tuple(SIZES.values())), tuple(SIZES))
    in_specs = (
        P(COL + ROW, None),
        P(),
        P(ROW, COL, None, None, None),
        P(ROW, COL, None),
        P(ROW, COL, None),
        P(ROW + COL, None),
        P(ROW + COL, None),
    )
    out_specs = (P(ROW + COL, None), P(COL + ROW, None), P())
    return jax.shard_map(shards, mesh=fine, in_specs=in_specs, out_specs=out_specs, check_vma=False)
```

```python
import math

import jax
import jax.numpy as jnp
from jax import lax
from jax.experimental import pallas as pl
from jax.experimental.pallas import tpu as pltpu
from jax.sharding import Mesh, PartitionSpec as P

SIZES = {"y": 8, "z": 4, "x": 4, "far": 3, "core": 2}
ROW = ("y", "z", "x")
COL = ("far", "core")
STEP = 4
VMEM = 48 * 1024 * 1024


def exchange(blocks, axes):
    return lax.all_to_all(blocks, axes, split_axis=0, concat_axis=0, tiled=True)


def spread(block, axes):
    count = math.prod(SIZES[axis] for axis in axes)
    return exchange(jnp.broadcast_to(block[None], (count,) + block.shape), axes)


def shift(block, axis, by):
    count = SIZES[axis]
    return lax.ppermute(block, axis, [(i, (i + by) % count) for i in range(count)])


def add(*blocks):
    return sum(block.astype(jnp.float32) for block in blocks).astype(jnp.bfloat16)


def forward_kernel(rows_of, cols_of, values, panel, pre, after, out, local_weight, total):
    tiles = values.shape[0]
    total[...] = jnp.zeros_like(total)

    @pl.loop(0, tiles // STEP)
    def _(turn):
        at = [turn * STEP + i for i in range(STEP)]
        prods = [
            jnp.dot(values[k], panel[cols_of[k]], preferred_element_type=jnp.float32)
            for k in at
        ]
        for k, prod in zip(at, prods):
            total[rows_of[k]] += prod

    share = jnp.zeros(local_weight.shape, jnp.float32)
    for r in range(total.shape[0]):
        value = total[r]
        high = value.astype(jnp.bfloat16)
        low = (value - high.astype(jnp.float32)).astype(jnp.bfloat16)
        for part in (high, low):
            share += lax.dot_general(
                part, pre[r], (((0,), (0,)), ((), ())), preferred_element_type=jnp.float32
            )
        out[r] = value
    local_weight[...] = share


def backward_kernel(here, rows_of, cols_of, values, weight, pre, *refs):
    *outs, grads, total = refs
    tiles = values.shape[0]
    total[...] = jnp.zeros_like(total)
    for r in range(pre.shape[0]):
        grads[r] = lax.dot_general(
            weight[...], pre[r], (((1,), (1,)), ((), ())), preferred_element_type=jnp.float32
        ).astype(jnp.bfloat16)

    @pl.loop(0, tiles // STEP)
    def _(turn):
        at = [turn * STEP + i for i in range(STEP)]
        prods = [
            jnp.dot(grads[rows_of[k]], values[k], preferred_element_type=jnp.float32)
            for k in at
        ]
        for k, prod in zip(at, prods):
            total[cols_of[k]] += prod

    inner = SIZES["x"]
    half = outs[0].shape[0]

    @pl.loop(0, half)
    def _(j):
        for ahead in range(inner):
            x = lax.rem(here[0] + ahead, inner)
            for part in range(2):
                block = (part * half + j) * inner + x
                outs[2 * ahead + part][j] = total[block].astype(jnp.bfloat16)


def call(kernel, scalars, operands, out_shape, scratch, flops, moved):
    whole = pl.BlockSpec(memory_space=pltpu.VMEM)
    index = pl.BlockSpec(memory_space=pltpu.SMEM)
    return pl.pallas_call(
        kernel,
        out_shape=out_shape,
        in_specs=[index] * len(scalars) + [whole] * len(operands),
        out_specs=jax.tree.map(lambda _: whole, out_shape),
        scratch_shapes=scratch,
        compiler_params=pltpu.CompilerParams(vmem_limit_bytes=VMEM),
        cost_estimate=pl.CostEstimate(flops=flops, bytes_accessed=moved, transcendentals=0),
    )(*scalars, *operands)


def shards(feats, weight, tile_values, tile_rows, tile_cols, relu_mask, grad_out):
    values = tile_values[0, 0]
    rows_of = tile_rows[0, 0]
    cols_of = tile_cols[0, 0]
    tiles, block, _ = values.shape
    owned, width = feats.shape
    row_count = math.prod(SIZES[axis] for axis in COL)
    col_count = math.prod(SIZES[axis] for axis in ROW)
    flops = 2 * tiles * block * block * width
    here = lax.axis_index("x").astype(jnp.int32).reshape(1)

    grad_pre = grad_out * relu_mask.astype(jnp.bfloat16)
    with jax.named_scope("gather_near"):
        near = spread(feats, ("z", "x"))
    with jax.named_scope("gather_grad"):
        pre = lax.all_gather(grad_pre, COL, axis=0, tiled=True).reshape(-1, block, width)
    near, pre = lax.optimization_barrier((near, pre))
    with jax.named_scope("gather_far"):
        panel = lax.all_gather(near.reshape(-1, width), "y", axis=0, tiled=True)
    panel = panel.reshape(col_count, block, width)

    half = col_count // SIZES["x"] // 2
    with jax.named_scope("backward"):
        sums = call(
            backward_kernel, (here, rows_of, cols_of), (values, weight, pre),
            (jax.ShapeDtypeStruct((half, width, block), jnp.bfloat16),) * (2 * SIZES["x"]),
            [
                pltpu.VMEM((row_count, width, block), jnp.bfloat16),
                pltpu.VMEM((col_count, width, block), jnp.float32),
            ],
            flops, 2 * values.size + 6 * col_count * block * width,
        )
    own, right, opposite, left = (sums[2 * i : 2 * i + 2] for i in range(SIZES["x"]))
    with jax.named_scope("scatter_x"):
        relay_right = shift(opposite[0], "x", 1)
        relay_left = shift(opposite[1], "x", -1)
        from_left_1 = shift(right[1], "x", 1)
        from_right_0 = shift(left[0], "x", -1)
        from_left_0 = shift(add(right[0], relay_right), "x", 1)
        from_right_1 = shift(add(left[1], relay_left), "x", -1)
        part = jnp.concatenate(
            [add(own[0], from_left_0, from_right_0), add(own[1], from_left_1, from_right_1)]
        )
    with jax.named_scope("scatter_yz"):
        got = exchange(part, ("y", "z"))

    with jax.named_scope("forward"):
        partial_value, local_weight = call(
            forward_kernel, (rows_of, cols_of), (values, panel, pre, part[0, :16]),
            (
                jax.ShapeDtypeStruct((row_count, block, width), jnp.float32),
                jax.ShapeDtypeStruct((width, width), jnp.float32),
            ),
            [pltpu.VMEM((row_count, block, width), jnp.float32)],
            flops, 2 * values.size + 2 * panel.size,
        )
    with jax.named_scope("scatter_col"):
        agg = lax.psum_scatter(
            partial_value.reshape(-1, width), COL, scatter_dimension=0, tiled=True
        ).astype(jnp.bfloat16)
    preact = jnp.dot(agg, weight, preferred_element_type=jnp.float32).astype(jnp.bfloat16)
    with jax.named_scope("weight_col"):
        local_weight = jnp.sum(
            lax.all_gather(local_weight, COL, axis=0, tiled=True).reshape(-1, width, width), axis=0
        )
    local_weight, got = lax.optimization_barrier((local_weight, got))
    grad_feats = jnp.sum(got.astype(jnp.float32), axis=0).T
    with jax.named_scope("weight_sum"):
        pieces = SIZES["z"] * SIZES["x"]
        piece = jnp.sum(exchange(local_weight.reshape(pieces, -1, width), ("z", "x")), axis=0)
        piece = jnp.sum(spread(piece, ("y",)), axis=0)
        grad_weight = spread(piece, ("z", "x")).reshape(width, width)
    total_nodes = owned * row_count * col_count
    grad_weight = grad_weight / jnp.sqrt(jnp.float32(total_nodes))
    return (preact, grad_feats, grad_weight)


def solution(mesh):
    fine = Mesh(mesh.devices.reshape(tuple(SIZES.values())), tuple(SIZES))
    in_specs = (
        P(COL + ROW, None),
        P(),
        P(ROW, COL, None, None, None),
        P(ROW, COL, None),
        P(ROW, COL, None),
        P(ROW + COL, None),
        P(ROW + COL, None),
    )
    out_specs = (P(ROW + COL, None), P(COL + ROW, None), P())
    return jax.shard_map(shards, mesh=fine, in_specs=in_specs, out_specs=out_specs, check_vma=False)
```

```python
import math

import jax
import jax.numpy as jnp
from jax import lax
from jax.experimental import pallas as pl
from jax.experimental.pallas import tpu as pltpu
from jax.sharding import Mesh, PartitionSpec as P

SIZES = {"y": 8, "z": 4, "x": 4, "far": 3, "core": 2}
ROW = ("y", "z", "x")
COL = ("far", "core")
STEP = 4
VMEM = 48 * 1024 * 1024


def exchange(blocks, axes):
    return lax.all_to_all(blocks, axes, split_axis=0, concat_axis=0, tiled=True)


def spread(block, axes):
    count = math.prod(SIZES[axis] for axis in axes)
    return exchange(jnp.broadcast_to(block[None], (count,) + block.shape), axes)


def shift(block, axis, by):
    count = SIZES[axis]
    return lax.ppermute(block, axis, [(i, (i + by) % count) for i in range(count)])


def add(*blocks):
    return sum(block.astype(jnp.float32) for block in blocks).astype(jnp.bfloat16)


def forward_kernel(rows_of, cols_of, values, panel, pre, after, out, local_weight, total):
    tiles = values.shape[0]
    total[...] = jnp.zeros_like(total)

    @pl.loop(0, tiles // STEP)
    def _(turn):
        at = [turn * STEP + i for i in range(STEP)]
        prods = [
            jnp.dot(values[k], panel[cols_of[k]], preferred_element_type=jnp.float32)
            for k in at
        ]
        for k, prod in zip(at, prods):
            total[rows_of[k]] += prod

    share = jnp.zeros(local_weight.shape, jnp.float32)
    for r in range(total.shape[0]):
        value = total[r]
        high = value.astype(jnp.bfloat16)
        low = (value - high.astype(jnp.float32)).astype(jnp.bfloat16)
        for part in (high, low):
            share += lax.dot_general(
                part, pre[r], (((0,), (0,)), ((), ())), preferred_element_type=jnp.float32
            )
        out[r] = value
    local_weight[...] = share


def backward_kernel(here, rows_of, cols_of, values, weight, pre, *refs):
    *outs, grads, total = refs
    tiles = values.shape[0]
    total[...] = jnp.zeros_like(total)
    for r in range(pre.shape[0]):
        grads[r] = lax.dot_general(
            weight[...], pre[r], (((1,), (1,)), ((), ())), preferred_element_type=jnp.float32
        ).astype(jnp.bfloat16)

    @pl.loop(0, tiles // STEP)
    def _(turn):
        at = [turn * STEP + i for i in range(STEP)]
        prods = [
            jnp.dot(grads[rows_of[k]], values[k], preferred_element_type=jnp.float32)
            for k in at
        ]
        for k, prod in zip(at, prods):
            total[cols_of[k]] += prod

    inner = SIZES["x"]
    half = outs[0].shape[0]

    @pl.loop(0, half)
    def _(j):
        for ahead in range(inner):
            x = lax.rem(here[0] + ahead, inner)
            for part in range(2):
                block = (part * half + j) * inner + x
                outs[2 * ahead + part][j] = total[block].astype(jnp.bfloat16)


def call(kernel, scalars, operands, out_shape, scratch, flops, moved):
    whole = pl.BlockSpec(memory_space=pltpu.VMEM)
    index = pl.BlockSpec(memory_space=pltpu.SMEM)
    return pl.pallas_call(
        kernel,
        out_shape=out_shape,
        in_specs=[index] * len(scalars) + [whole] * len(operands),
        out_specs=jax.tree.map(lambda _: whole, out_shape),
        scratch_shapes=scratch,
        compiler_params=pltpu.CompilerParams(vmem_limit_bytes=VMEM),
        cost_estimate=pl.CostEstimate(flops=flops, bytes_accessed=moved, transcendentals=0),
    )(*scalars, *operands)


def shards(feats, weight, tile_values, tile_rows, tile_cols, relu_mask, grad_out):
    values = tile_values[0, 0]
    rows_of = tile_rows[0, 0]
    cols_of = tile_cols[0, 0]
    tiles, block, _ = values.shape
    owned, width = feats.shape
    row_count = math.prod(SIZES[axis] for axis in COL)
    col_count = math.prod(SIZES[axis] for axis in ROW)
    flops = 2 * tiles * block * block * width
    here = lax.axis_index("x").astype(jnp.int32).reshape(1)

    grad_pre = grad_out * relu_mask.astype(jnp.bfloat16)
    def both(block):
        other = shift(block, "core", 1)
        first = lax.axis_index("core") == 0
        return jnp.stack([jnp.where(first, block, other), jnp.where(first, other, block)])

    with jax.named_scope("gather_grad"):
        pair = both(grad_pre)
        feats, pair = lax.optimization_barrier((feats, pair))
    with jax.named_scope("gather_near"):
        near = spread(feats, ("z", "x"))
    with jax.named_scope("gather_grad"):
        pre = lax.all_gather(pair, "far", axis=0, tiled=True)
    near, pre = lax.optimization_barrier((near, pre))
    with jax.named_scope("gather_far"):
        panel = lax.all_gather(near.reshape(-1, width), "y", axis=0, tiled=True)
    panel = panel.reshape(col_count, block, width)

    half = col_count // SIZES["x"] // 2
    with jax.named_scope("backward"):
        sums = call(
            backward_kernel, (here, rows_of, cols_of), (values, weight, pre),
            (jax.ShapeDtypeStruct((half, width, block), jnp.bfloat16),) * (2 * SIZES["x"]),
            [
                pltpu.VMEM((row_count, width, block), jnp.bfloat16),
                pltpu.VMEM((col_count, width, block), jnp.float32),
            ],
            flops, 2 * values.size + 6 * col_count * block * width,
        )
    own, right, opposite, left = (sums[2 * i : 2 * i + 2] for i in range(SIZES["x"]))
    with jax.named_scope("scatter_x"):
        relay_right = shift(opposite[0], "x", 1)
        relay_left = shift(opposite[1], "x", -1)
        from_left_1 = shift(right[1], "x", 1)
        from_right_0 = shift(left[0], "x", -1)
        from_left_0 = shift(add(right[0], relay_right), "x", 1)
        from_right_1 = shift(add(left[1], relay_left), "x", -1)
        part = jnp.concatenate(
            [add(own[0], from_left_0, from_right_0), add(own[1], from_left_1, from_right_1)]
        )

    with jax.named_scope("forward"):
        partial_value, local_weight = call(
            forward_kernel, (rows_of, cols_of), (values, panel, pre, part[0, :16]),
            (
                jax.ShapeDtypeStruct((row_count, block, width), jnp.float32),
                jax.ShapeDtypeStruct((width, width), jnp.float32),
            ),
            [pltpu.VMEM((row_count, block, width), jnp.float32)],
            flops, 2 * values.size + 2 * panel.size,
        )
    with jax.named_scope("scatter_col"):
        agg = lax.psum_scatter(
            partial_value.reshape(-1, width), COL, scatter_dimension=0, tiled=True
        ).astype(jnp.bfloat16)
    preact = jnp.dot(agg, weight, preferred_element_type=jnp.float32).astype(jnp.bfloat16)
    with jax.named_scope("scatter_yz"):
        local_weight, part = lax.optimization_barrier((local_weight, part))
        got = exchange(part, ("y", "z"))
    with jax.named_scope("weight_sum"):
        grad_weight = local_weight + shift(local_weight, "core", 1)
        for axis in ("far", "x", "z"):
            grad_weight = jnp.sum(lax.all_gather(grad_weight, axis, axis=0), axis=0)
        grad_weight, got = lax.optimization_barrier((grad_weight, got))
        grad_weight = jnp.sum(spread(grad_weight, ("y",)), axis=0)
    grad_feats = jnp.sum(got.astype(jnp.float32), axis=0).T
    total_nodes = owned * row_count * col_count
    grad_weight = grad_weight / jnp.sqrt(jnp.float32(total_nodes))
    return (preact, grad_feats, grad_weight)


def solution(mesh):
    fine = Mesh(mesh.devices.reshape(tuple(SIZES.values())), tuple(SIZES))
    in_specs = (
        P(COL + ROW, None),
        P(),
        P(ROW, COL, None, None, None),
        P(ROW, COL, None),
        P(ROW, COL, None),
        P(ROW + COL, None),
        P(ROW + COL, None),
    )
    out_specs = (P(ROW + COL, None), P(COL + ROW, None), P())
    return jax.shard_map(shards, mesh=fine, in_specs=in_specs, out_specs=out_specs, check_vma=False)
```

```python
import math

import jax
import jax.numpy as jnp
from jax import lax
from jax.experimental import pallas as pl
from jax.experimental.pallas import tpu as pltpu
from jax.sharding import Mesh, PartitionSpec as P

SIZES = {"y": 8, "z": 4, "x": 4, "far": 3, "core": 2}
ROW = ("y", "z", "x")
COL = ("far", "core")
STEP = 4
VMEM = 48 * 1024 * 1024


def exchange(blocks, axes):
    return lax.all_to_all(blocks, axes, split_axis=0, concat_axis=0, tiled=True)


def spread(block, axes):
    count = math.prod(SIZES[axis] for axis in axes)
    return exchange(jnp.broadcast_to(block[None], (count,) + block.shape), axes)


def shift(block, axis, by):
    count = SIZES[axis]
    return lax.ppermute(block, axis, [(i, (i + by) % count) for i in range(count)])


def add(*blocks):
    return sum(block.astype(jnp.float32) for block in blocks).astype(jnp.bfloat16)


def forward_kernel(index, values, panel, pre, after, out, local_weight, total):
    tiles = values.shape[0]
    total[...] = jnp.zeros_like(total)

    @pl.loop(0, tiles // STEP)
    def _(turn):
        at = [turn * STEP + i for i in range(STEP)]
        prods = [
            jnp.dot(values[k], panel[index[tiles + k]], preferred_element_type=jnp.float32)
            for k in at
        ]
        for k, prod in zip(at, prods):
            total[index[k]] += prod

    share = jnp.zeros(local_weight.shape, jnp.float32)
    for r in range(total.shape[0]):
        value = total[r]
        high = value.astype(jnp.bfloat16)
        low = (value - high.astype(jnp.float32)).astype(jnp.bfloat16)
        for part in (high, low):
            share += lax.dot_general(
                part, pre[r], (((0,), (0,)), ((), ())), preferred_element_type=jnp.float32
            )
        out[r] = value
    local_weight[...] = share


def backward_kernel(index, values, weight, pre, *refs):
    *outs, grads, total = refs
    tiles = values.shape[0]
    total[...] = jnp.zeros_like(total)
    for r in range(pre.shape[0]):
        grads[r] = lax.dot_general(
            weight[...], pre[r], (((1,), (1,)), ((), ())), preferred_element_type=jnp.float32
        ).astype(jnp.bfloat16)

    @pl.loop(0, tiles // STEP)
    def _(turn):
        at = [turn * STEP + i for i in range(STEP)]
        prods = [
            jnp.dot(grads[index[k]], values[k], preferred_element_type=jnp.float32)
            for k in at
        ]
        for k, prod in zip(at, prods):
            total[index[tiles + k]] += prod

    inner = SIZES["x"]
    half = outs[0].shape[0]

    @pl.loop(0, half)
    def _(j):
        for ahead in range(inner):
            x = lax.rem(index[2 * values.shape[0]] + ahead, inner)
            for part in range(2):
                block = (part * half + j) * inner + x
                outs[2 * ahead + part][j] = total[block].astype(jnp.bfloat16)


def call(kernel, index, operands, out_shape, scratch, flops, moved):
    whole = pl.BlockSpec(memory_space=pltpu.VMEM)
    return pl.pallas_call(
        kernel,
        out_shape=out_shape,
        in_specs=[pl.BlockSpec(memory_space=pltpu.SMEM)] + [whole] * len(operands),
        out_specs=jax.tree.map(lambda _: whole, out_shape),
        scratch_shapes=scratch,
        compiler_params=pltpu.CompilerParams(vmem_limit_bytes=VMEM),
        cost_estimate=pl.CostEstimate(flops=flops, bytes_accessed=moved, transcendentals=0),
    )(index, *operands)


def shards(feats, weight, tile_values, tile_rows, tile_cols, relu_mask, grad_out):
    values = tile_values[0, 0]
    tiles, block, _ = values.shape
    owned, width = feats.shape
    row_count = math.prod(SIZES[axis] for axis in COL)
    col_count = math.prod(SIZES[axis] for axis in ROW)
    flops = 2 * tiles * block * block * width
    here = lax.axis_index("x").astype(jnp.int32).reshape(1)
    index = jnp.concatenate([tile_rows[0, 0], tile_cols[0, 0], here])

    grad_pre = grad_out * relu_mask.astype(jnp.bfloat16)
    with jax.named_scope("gather_near"):
        near = spread(feats, ("z", "x"))
    with jax.named_scope("gather_grad"):
        grad_pre, near = lax.optimization_barrier((grad_pre, near))
        pre = lax.all_gather(grad_pre, COL, axis=0, tiled=True).reshape(-1, block, width)
    with jax.named_scope("gather_far"):
        panel = lax.all_gather(near.reshape(-1, width), "y", axis=0, tiled=True)
    panel = panel.reshape(col_count, block, width)

    half = col_count // SIZES["x"] // 2
    with jax.named_scope("backward"):
        sums = call(
            backward_kernel, index, (values, weight, pre),
            (jax.ShapeDtypeStruct((half, width, block), jnp.bfloat16),) * (2 * SIZES["x"]),
            [
                pltpu.VMEM((row_count, width, block), jnp.bfloat16),
                pltpu.VMEM((col_count, width, block), jnp.float32),
            ],
            flops, 2 * values.size + 6 * col_count * block * width,
        )
    own, right, opposite, left = (sums[2 * i : 2 * i + 2] for i in range(SIZES["x"]))
    with jax.named_scope("scatter_x"):
        relay_right = shift(opposite[0], "x", 1)
        relay_left = shift(opposite[1], "x", -1)
        from_left_1 = shift(right[1], "x", 1)
        from_right_0 = shift(left[0], "x", -1)
        relays = add(right[0], relay_right), add(left[1], relay_left)
        from_left_0, from_right_1 = shift(relays[0], "x", 1), shift(relays[1], "x", -1)

    with jax.named_scope("forward"):
        partial_value, local_weight = call(
            forward_kernel, index, (values, panel, pre, relays[0][0, :16] + relays[1][0, :16]),
            (
                jax.ShapeDtypeStruct((row_count, block, width), jnp.float32),
                jax.ShapeDtypeStruct((width, width), jnp.float32),
            ),
            [pltpu.VMEM((row_count, block, width), jnp.float32)],
            flops, 2 * values.size + 2 * panel.size,
        )
    *own, local_weight = lax.optimization_barrier((*own, local_weight))
    with jax.named_scope("scatter_x"):
        part = jnp.concatenate(
            [add(own[0], from_left_0, from_right_0), add(own[1], from_left_1, from_right_1)]
        )
    with jax.named_scope("scatter_yz"):
        got = exchange(part, ("y", "z"))
    with jax.named_scope("scatter_col"):
        agg = lax.psum_scatter(
            partial_value.reshape(-1, width), COL, scatter_dimension=0, tiled=True
        ).astype(jnp.bfloat16)
    preact = jnp.dot(agg, weight, preferred_element_type=jnp.float32).astype(jnp.bfloat16)
    with jax.named_scope("weight_col"):
        local_weight = jnp.sum(
            lax.all_gather(local_weight, COL, axis=0, tiled=True).reshape(-1, width, width), axis=0
        )
    local_weight, got = lax.optimization_barrier((local_weight, got))
    grad_feats = jnp.sum(got.astype(jnp.float32), axis=0).T
    with jax.named_scope("weight_sum"):
        pieces = SIZES["z"] * SIZES["x"]
        piece = jnp.sum(exchange(local_weight.reshape(pieces, -1, width), ("z", "x")), axis=0)
        piece = jnp.sum(spread(piece, ("y",)), axis=0)
        grad_weight = spread(piece, ("z", "x")).reshape(width, width)
    total_nodes = owned * row_count * col_count
    grad_weight = grad_weight / jnp.sqrt(jnp.float32(total_nodes))
    return (preact, grad_feats, grad_weight)


def solution(mesh):
    fine = Mesh(mesh.devices.reshape(tuple(SIZES.values())), tuple(SIZES))
    in_specs = (
        P(COL + ROW, None),
        P(),
        P(ROW, COL, None, None, None),
        P(ROW, COL, None),
        P(ROW, COL, None),
        P(ROW + COL, None),
        P(ROW + COL, None),
    )
    out_specs = (P(ROW + COL, None), P(COL + ROW, None), P())
    return jax.shard_map(shards, mesh=fine, in_specs=in_specs, out_specs=out_specs, check_vma=False)
```

```python
import math

import jax
import jax.numpy as jnp
from jax import lax
from jax.experimental import pallas as pl
from jax.experimental.pallas import tpu as pltpu
from jax.sharding import Mesh, PartitionSpec as P

SIZES = {"y": 8, "z": 4, "x": 4, "far": 3, "core": 2}
ROW = ("y", "z", "x")
COL = ("far", "core")
STEP = 16
VMEM = 48 * 1024 * 1024


def exchange(blocks, axes):
    return lax.all_to_all(blocks, axes, split_axis=0, concat_axis=0, tiled=True)


def spread(block, axes):
    count = math.prod(SIZES[axis] for axis in axes)
    return exchange(jnp.broadcast_to(block[None], (count,) + block.shape), axes)


def shift(block, by):
    count = SIZES["x"]
    return lax.ppermute(block, "x", [(i, (i + by) % count) for i in range(count)])


def add(*blocks):
    return sum(block.astype(jnp.float32) for block in blocks).astype(jnp.bfloat16)


def forward_kernel(rows_of, cols_of, values, panel, pre, after, out, local_weight, total):
    tiles = values.shape[0]
    total[...] = jnp.zeros_like(total)

    @pl.loop(0, tiles // STEP)
    def _(turn):
        at = [turn * STEP + i for i in range(STEP)]
        prods = [
            jnp.dot(values[k], panel[cols_of[k]], preferred_element_type=jnp.float32)
            for k in at
        ]
        for k, prod in zip(at, prods):
            total[rows_of[k]] += prod

    share = jnp.zeros(local_weight.shape, jnp.float32)
    for r in range(total.shape[0]):
        value = total[r]
        high = value.astype(jnp.bfloat16)
        low = (value - high.astype(jnp.float32)).astype(jnp.bfloat16)
        for part in (high, low):
            share += lax.dot_general(
                part, pre[r], (((0,), (0,)), ((), ())), preferred_element_type=jnp.float32
            )
        out[r] = value
    local_weight[...] = share


def backward_kernel(here, rows_of, cols_of, values, pre, weight, *refs):
    *outs, after, grads, total = refs
    tiles = values.shape[0]
    total[...] = jnp.zeros_like(total)
    for r in range(pre.shape[0]):
        grads[r] = lax.dot_general(
            weight[...], pre[r], (((1,), (1,)), ((), ())), preferred_element_type=jnp.float32
        ).astype(jnp.bfloat16)

    @pl.loop(0, tiles // STEP)
    def _(turn):
        at = [turn * STEP + i for i in range(STEP)]
        prods = [
            jnp.dot(grads[rows_of[k]], values[k], preferred_element_type=jnp.float32)
            for k in at
        ]
        for k, prod in zip(at, prods):
            total[cols_of[k]] += prod

    inner = SIZES["x"]
    half = outs[0].shape[0]

    @pl.loop(0, half)
    def _(j):
        for ahead in range(inner):
            x = lax.rem(here[0] + ahead, inner)
            for part in range(2):
                block = total[(part * half + j) * inner + x]
                outs[2 * ahead + part][j] = block.astype(jnp.bfloat16)

    after[...] = jnp.zeros_like(after)


def call(kernel, scalars, operands, out_shape, scratch, flops, moved):
    whole = pl.BlockSpec(memory_space=pltpu.VMEM)
    index = pl.BlockSpec(memory_space=pltpu.SMEM)
    return pl.pallas_call(
        kernel,
        out_shape=out_shape,
        in_specs=[index] * len(scalars) + [whole] * len(operands),
        out_specs=jax.tree.map(lambda _: whole, out_shape),
        scratch_shapes=scratch,
        compiler_params=pltpu.CompilerParams(vmem_limit_bytes=VMEM),
        cost_estimate=pl.CostEstimate(flops=flops, bytes_accessed=moved, transcendentals=0),
    )(*scalars, *operands)


def shards(feats, weight, tile_values, tile_rows, tile_cols, relu_mask, grad_out):
    values = tile_values[0, 0]
    rows_of = tile_rows[0, 0]
    cols_of = tile_cols[0, 0]
    tiles, block, _ = values.shape
    owned, width = feats.shape
    row_count = math.prod(SIZES[axis] for axis in COL)
    col_count = math.prod(SIZES[axis] for axis in ROW)
    flops = 2 * tiles * block * block * width

    with jax.named_scope("gather_near"):
        near = spread(feats, ("z", "x"))
    with jax.named_scope("gather_far"):
        panel = lax.all_gather(near.reshape(-1, width), "y", axis=0, tiled=True)
    panel = panel.reshape(col_count, block, width)

    grad_pre = grad_out * relu_mask.astype(jnp.bfloat16)
    with jax.named_scope("gather_grad"):
        pre = lax.all_gather(grad_pre, COL, axis=0, tiled=True).reshape(-1, block, width)

    here = lax.axis_index("x").astype(jnp.int32).reshape(1)
    half = col_count // SIZES["x"] // 2
    with jax.named_scope("backward"):
        *sums, after = call(
            backward_kernel, (here, rows_of, cols_of), (values, pre, weight),
            (jax.ShapeDtypeStruct((half, width, block), jnp.bfloat16),) * (2 * SIZES["x"])
            + (jax.ShapeDtypeStruct((8, 128), jnp.float32),),
            [
                pltpu.VMEM((row_count, width, block), jnp.bfloat16),
                pltpu.VMEM((col_count, width, block), jnp.float32),
            ],
            flops, 2 * values.size + 6 * col_count * block * width,
        )
    with jax.named_scope("scatter_x"):
        own, right, opposite, left = (sums[2 * i : 2 * i + 2] for i in range(SIZES["x"]))
        relay_right = shift(opposite[0], 1)
        relay_left = shift(opposite[1], -1)
        from_left_1 = shift(right[1], 1)
        from_right_0 = shift(left[0], -1)
        from_left_0 = shift(add(right[0], relay_right), 1)
        from_right_1 = shift(add(left[1], relay_left), -1)
        part = jnp.concatenate(
            [add(own[0], from_left_0, from_right_0), add(own[1], from_left_1, from_right_1)]
        )
    with jax.named_scope("scatter_yz"):
        got = exchange(part, ("y", "z"))
        grad_feats = jnp.sum(got.astype(jnp.float32), axis=0).T

    with jax.named_scope("forward"):
        partial_value, local_weight = call(
            forward_kernel, (rows_of, cols_of), (values, panel, pre, after),
            (
                jax.ShapeDtypeStruct((row_count, block, width), jnp.float32),
                jax.ShapeDtypeStruct((width, width), jnp.float32),
            ),
            [pltpu.VMEM((row_count, block, width), jnp.float32)],
            flops, 2 * values.size + 2 * panel.size,
        )
    with jax.named_scope("scatter_col"):
        agg = lax.psum_scatter(
            partial_value.reshape(-1, width), COL, scatter_dimension=0, tiled=True
        ).astype(jnp.bfloat16)
    preact = jnp.dot(agg, weight, preferred_element_type=jnp.float32).astype(jnp.bfloat16)

    with jax.named_scope("weight_sum"):
        near_axes, far_axes = ("z", "x", "core"), ("y", "far")
        pieces = math.prod(SIZES[axis] for axis in near_axes)
        piece = jnp.sum(exchange(local_weight.reshape(pieces, -1, width), near_axes), axis=0)
        piece = jnp.sum(spread(piece, far_axes), axis=0)
        grad_weight = spread(piece, near_axes).reshape(width, width)
    total_nodes = owned * row_count * col_count
    grad_weight = grad_weight / jnp.sqrt(jnp.float32(total_nodes))
    return (preact, grad_feats, grad_weight)


def solution(mesh):
    fine = Mesh(mesh.devices.reshape(tuple(SIZES.values())), tuple(SIZES))
    in_specs = (
        P(COL + ROW, None),
        P(),
        P(ROW, COL, None, None, None),
        P(ROW, COL, None),
        P(ROW, COL, None),
        P(ROW + COL, None),
        P(ROW + COL, None),
    )
    out_specs = (P(ROW + COL, None), P(COL + ROW, None), P())
    return jax.shard_map(shards, mesh=fine, in_specs=in_specs, out_specs=out_specs, check_vma=False)
```

```python
import math

import jax
import jax.numpy as jnp
from jax import lax
from jax.experimental import pallas as pl
from jax.experimental.pallas import tpu as pltpu
from jax.sharding import Mesh, PartitionSpec as P

SIZES = {"y": 8, "z": 4, "x": 4, "far": 3, "core": 2}
ROW = ("y", "z", "x")
COL = ("far", "core")
STEP = 16
VMEM = 48 * 1024 * 1024


def exchange(blocks, axes):
    return lax.all_to_all(blocks, axes, split_axis=0, concat_axis=0, tiled=True)


def spread(block, axes):
    count = math.prod(SIZES[axis] for axis in axes)
    return exchange(jnp.broadcast_to(block[None], (count,) + block.shape), axes)


def shift(block, by):
    count = SIZES["x"]
    return lax.ppermute(block, "x", [(i, (i + by) % count) for i in range(count)])


def add(*blocks):
    return sum(block.astype(jnp.float32) for block in blocks).astype(jnp.bfloat16)


def forward_kernel(rows_of, cols_of, values, panel, pre, after, out, local_weight, total):
    tiles = values.shape[0]
    total[...] = jnp.zeros_like(total)

    @pl.loop(0, tiles // STEP)
    def _(turn):
        at = [turn * STEP + i for i in range(STEP)]
        prods = [
            jnp.dot(values[k], panel[cols_of[k]], preferred_element_type=jnp.float32)
            for k in at
        ]
        for k, prod in zip(at, prods):
            total[rows_of[k]] += prod

    share = jnp.zeros(local_weight.shape, jnp.float32)
    for r in range(total.shape[0]):
        value = total[r]
        high = value.astype(jnp.bfloat16)
        low = (value - high.astype(jnp.float32)).astype(jnp.bfloat16)
        for part in (high, low):
            share += lax.dot_general(
                part, pre[r], (((0,), (0,)), ((), ())), preferred_element_type=jnp.float32
            )
        out[r] = value
    local_weight[...] = share


def backward_kernel(here, rows_of, cols_of, values, pre, weight, *refs):
    *outs, after, grads, total = refs
    tiles = values.shape[0]
    total[...] = jnp.zeros_like(total)
    for r in range(pre.shape[0]):
        grads[r] = lax.dot_general(
            weight[...], pre[r], (((1,), (1,)), ((), ())), preferred_element_type=jnp.float32
        ).astype(jnp.bfloat16)

    @pl.loop(0, tiles // STEP)
    def _(turn):
        at = [turn * STEP + i for i in range(STEP)]
        prods = [
            jnp.dot(grads[rows_of[k]], values[k], preferred_element_type=jnp.float32)
            for k in at
        ]
        for k, prod in zip(at, prods):
            total[cols_of[k]] += prod

    inner = SIZES["x"]
    half = outs[0].shape[0]

    @pl.loop(0, half)
    def _(j):
        for ahead in range(inner):
            x = lax.rem(here[0] + ahead, inner)
            for part in range(2):
                block = total[(part * half + j) * inner + x]
                outs[2 * ahead + part][j] = block.astype(jnp.bfloat16)

    after[...] = jnp.zeros_like(after)


def call(kernel, scalars, operands, out_shape, scratch, flops, moved):
    whole = pl.BlockSpec(memory_space=pltpu.VMEM)
    index = pl.BlockSpec(memory_space=pltpu.SMEM)
    return pl.pallas_call(
        kernel,
        out_shape=out_shape,
        in_specs=[index] * len(scalars) + [whole] * len(operands),
        out_specs=jax.tree.map(lambda _: whole, out_shape),
        scratch_shapes=scratch,
        compiler_params=pltpu.CompilerParams(vmem_limit_bytes=VMEM),
        cost_estimate=pl.CostEstimate(flops=flops, bytes_accessed=moved, transcendentals=0),
    )(*scalars, *operands)


def shards(feats, weight, tile_values, tile_rows, tile_cols, relu_mask, grad_out):
    values = tile_values[0, 0]
    rows_of = tile_rows[0, 0]
    cols_of = tile_cols[0, 0]
    tiles, block, _ = values.shape
    owned, width = feats.shape
    row_count = math.prod(SIZES[axis] for axis in COL)
    col_count = math.prod(SIZES[axis] for axis in ROW)
    flops = 2 * tiles * block * block * width

    with jax.named_scope("gather_near"):
        near = spread(feats, ("z", "x"))
    with jax.named_scope("gather_far"):
        panel = lax.all_gather(near.reshape(-1, width), "y", axis=0, tiled=True)
    panel = panel.reshape(col_count, block, width)

    grad_pre = grad_out * relu_mask.astype(jnp.bfloat16)
    with jax.named_scope("gather_grad"):
        pre = lax.all_gather(grad_pre, COL, axis=0, tiled=True).reshape(-1, block, width)

    here = lax.axis_index("x").astype(jnp.int32).reshape(1)
    half = col_count // SIZES["x"] // 2
    with jax.named_scope("backward"):
        *sums, after = call(
            backward_kernel, (here, rows_of, cols_of), (values, pre, weight),
            (jax.ShapeDtypeStruct((half, width, block), jnp.bfloat16),) * (2 * SIZES["x"])
            + (jax.ShapeDtypeStruct((8, 128), jnp.float32),),
            [
                pltpu.VMEM((row_count, width, block), jnp.bfloat16),
                pltpu.VMEM((col_count, width, block), jnp.float32),
            ],
            flops, 2 * values.size + 6 * col_count * block * width,
        )
    with jax.named_scope("scatter_x"):
        own, right, opposite, left = (sums[2 * i : 2 * i + 2] for i in range(SIZES["x"]))
        relay_right = shift(opposite[0], 1)
        relay_left = shift(opposite[1], -1)
        from_left_1 = shift(right[1], 1)
        from_right_0 = shift(left[0], -1)
        from_left_0 = shift(add(right[0], relay_right), 1)
        from_right_1 = shift(add(left[1], relay_left), -1)
        part = jnp.concatenate(
            [add(own[0], from_left_0, from_right_0), add(own[1], from_left_1, from_right_1)]
        )
    with jax.named_scope("scatter_yz"):
        got = exchange(part, ("y", "z"))

    with jax.named_scope("forward"):
        partial_value, local_weight = call(
            forward_kernel, (rows_of, cols_of), (values, panel, pre, after),
            (
                jax.ShapeDtypeStruct((row_count, block, width), jnp.float32),
                jax.ShapeDtypeStruct((width, width), jnp.float32),
            ),
            [pltpu.VMEM((row_count, block, width), jnp.float32)],
            flops, 2 * values.size + 2 * panel.size,
        )
    with jax.named_scope("scatter_col"):
        agg = lax.psum_scatter(
            partial_value.reshape(-1, width), COL, scatter_dimension=0, tiled=True
        ).astype(jnp.bfloat16)
    preact = jnp.dot(agg, weight, preferred_element_type=jnp.float32).astype(jnp.bfloat16)

    with jax.named_scope("weight_sum"):
        near_axes, far_axes = ("z", "x", "core"), ("y", "far")
        pieces = math.prod(SIZES[axis] for axis in near_axes)
        piece = jnp.sum(exchange(local_weight.reshape(pieces, -1, width), near_axes), axis=0)
        piece, got = lax.optimization_barrier((piece, got))
        piece = jnp.sum(spread(piece, far_axes), axis=0)
        grad_weight = spread(piece, near_axes).reshape(width, width)
    grad_feats = jnp.sum(got.astype(jnp.float32), axis=0).T
    total_nodes = owned * row_count * col_count
    grad_weight = grad_weight / jnp.sqrt(jnp.float32(total_nodes))
    return (preact, grad_feats, grad_weight)


def solution(mesh):
    fine = Mesh(mesh.devices.reshape(tuple(SIZES.values())), tuple(SIZES))
    in_specs = (
        P(COL + ROW, None),
        P(),
        P(ROW, COL, None, None, None),
        P(ROW, COL, None),
        P(ROW, COL, None),
        P(ROW + COL, None),
        P(ROW + COL, None),
    )
    out_specs = (P(ROW + COL, None), P(COL + ROW, None), P())
    return jax.shard_map(shards, mesh=fine, in_specs=in_specs, out_specs=out_specs, check_vma=False)
```

```python
import math

import jax
import jax.numpy as jnp
from jax import lax
from jax.experimental import pallas as pl
from jax.experimental.pallas import tpu as pltpu
from jax.sharding import Mesh, PartitionSpec as P

SIZES = {"y": 8, "z": 4, "x": 4, "far": 3, "core": 2}
ROW = ("y", "z", "x")
COL = ("far", "core")
STEP = 32
VMEM = 48 * 1024 * 1024


def exchange(blocks, axes):
    return lax.all_to_all(blocks, axes, split_axis=0, concat_axis=0, tiled=True)


def spread(block, axes):
    count = math.prod(SIZES[axis] for axis in axes)
    return exchange(jnp.broadcast_to(block[None], (count,) + block.shape), axes)


def shift(block, by):
    count = SIZES["x"]
    return lax.ppermute(block, "x", [(i, (i + by) % count) for i in range(count)])


def add(*blocks):
    return sum(block.astype(jnp.float32) for block in blocks).astype(jnp.bfloat16)


def forward_kernel(rows_of, cols_of, values, panel, pre, after, out, local_weight, total):
    tiles = values.shape[0]
    total[...] = jnp.zeros_like(total)

    @pl.loop(0, tiles // STEP)
    def _(turn):
        at = [turn * STEP + i for i in range(STEP)]
        prods = [
            jnp.dot(values[k], panel[cols_of[k]], preferred_element_type=jnp.float32)
            for k in at
        ]
        for k, prod in zip(at, prods):
            total[rows_of[k]] += prod

    share = jnp.zeros(local_weight.shape, jnp.float32)
    for r in range(total.shape[0]):
        value = total[r]
        high = value.astype(jnp.bfloat16)
        low = (value - high.astype(jnp.float32)).astype(jnp.bfloat16)
        for part in (high, low):
            share += lax.dot_general(
                part, pre[r], (((0,), (0,)), ((), ())), preferred_element_type=jnp.float32
            )
        out[r] = value
    local_weight[...] = share


def backward_kernel(here, rows_of, cols_of, values, pre, weight, *refs):
    *outs, after, grads, total = refs
    tiles = values.shape[0]
    total[...] = jnp.zeros_like(total)
    for r in range(pre.shape[0]):
        grads[r] = lax.dot_general(
            weight[...], pre[r], (((1,), (1,)), ((), ())), preferred_element_type=jnp.float32
        ).astype(jnp.bfloat16)

    @pl.loop(0, tiles // STEP)
    def _(turn):
        at = [turn * STEP + i for i in range(STEP)]
        prods = [
            jnp.dot(grads[rows_of[k]], values[k], preferred_element_type=jnp.float32)
            for k in at
        ]
        for k, prod in zip(at, prods):
            total[cols_of[k]] += prod

    inner = SIZES["x"]
    half = outs[0].shape[0]

    @pl.loop(0, half)
    def _(j):
        for ahead in range(inner):
            x = lax.rem(here[0] + ahead, inner)
            for part in range(2):
                block = total[(part * half + j) * inner + x]
                outs[2 * ahead + part][j] = block.astype(jnp.bfloat16)

    after[...] = jnp.zeros_like(after)


def call(kernel, scalars, operands, out_shape, scratch, flops, moved):
    whole = pl.BlockSpec(memory_space=pltpu.VMEM)
    index = pl.BlockSpec(memory_space=pltpu.SMEM)
    return pl.pallas_call(
        kernel,
        out_shape=out_shape,
        in_specs=[index] * len(scalars) + [whole] * len(operands),
        out_specs=jax.tree.map(lambda _: whole, out_shape),
        scratch_shapes=scratch,
        compiler_params=pltpu.CompilerParams(vmem_limit_bytes=VMEM),
        cost_estimate=pl.CostEstimate(flops=flops, bytes_accessed=moved, transcendentals=0),
    )(*scalars, *operands)


def shards(feats, weight, tile_values, tile_rows, tile_cols, relu_mask, grad_out):
    values = tile_values[0, 0]
    rows_of = tile_rows[0, 0]
    cols_of = tile_cols[0, 0]
    tiles, block, _ = values.shape
    owned, width = feats.shape
    row_count = math.prod(SIZES[axis] for axis in COL)
    col_count = math.prod(SIZES[axis] for axis in ROW)
    flops = 2 * tiles * block * block * width

    with jax.named_scope("gather_near"):
        near = spread(feats, ("z", "x"))
    with jax.named_scope("gather_far"):
        panel = lax.all_gather(near.reshape(-1, width), "y", axis=0, tiled=True)
    panel = panel.reshape(col_count, block, width)

    grad_pre = grad_out * relu_mask.astype(jnp.bfloat16)
    with jax.named_scope("gather_grad"):
        pre = lax.all_gather(grad_pre, COL, axis=0, tiled=True).reshape(-1, block, width)

    here = lax.axis_index("x").astype(jnp.int32).reshape(1)
    half = col_count // SIZES["x"] // 2
    with jax.named_scope("backward"):
        *sums, after = call(
            backward_kernel, (here, rows_of, cols_of), (values, pre, weight),
            (jax.ShapeDtypeStruct((half, width, block), jnp.bfloat16),) * (2 * SIZES["x"])
            + (jax.ShapeDtypeStruct((8, 128), jnp.float32),),
            [
                pltpu.VMEM((row_count, width, block), jnp.bfloat16),
                pltpu.VMEM((col_count, width, block), jnp.float32),
            ],
            flops, 2 * values.size + 6 * col_count * block * width,
        )
    with jax.named_scope("scatter_x"):
        own, right, opposite, left = (sums[2 * i : 2 * i + 2] for i in range(SIZES["x"]))
        relay_right = shift(opposite[0], 1)
        relay_left = shift(opposite[1], -1)
        from_left_1 = shift(right[1], 1)
        from_right_0 = shift(left[0], -1)
        from_left_0 = shift(add(right[0], relay_right), 1)
        from_right_1 = shift(add(left[1], relay_left), -1)
        part = jnp.concatenate(
            [add(own[0], from_left_0, from_right_0), add(own[1], from_left_1, from_right_1)]
        )
    with jax.named_scope("scatter_yz"):
        got = exchange(part, ("y", "z"))

    with jax.named_scope("forward"):
        partial_value, local_weight = call(
            forward_kernel, (rows_of, cols_of), (values, panel, pre, after),
            (
                jax.ShapeDtypeStruct((row_count, block, width), jnp.float32),
                jax.ShapeDtypeStruct((width, width), jnp.float32),
            ),
            [pltpu.VMEM((row_count, block, width), jnp.float32)],
            flops, 2 * values.size + 2 * panel.size,
        )
    with jax.named_scope("scatter_col"):
        agg = lax.psum_scatter(
            partial_value.reshape(-1, width), COL, scatter_dimension=0, tiled=True
        ).astype(jnp.bfloat16)
    preact = jnp.dot(agg, weight, preferred_element_type=jnp.float32).astype(jnp.bfloat16)

    with jax.named_scope("weight_sum"):
        near_axes, far_axes = ("z", "x", "core"), ("y", "far")
        pieces = math.prod(SIZES[axis] for axis in near_axes)
        piece = jnp.sum(exchange(local_weight.reshape(pieces, -1, width), near_axes), axis=0)
        piece, got = lax.optimization_barrier((piece, got))
        piece = jnp.sum(spread(piece, far_axes), axis=0)
        grad_weight = spread(piece, near_axes).reshape(width, width)
    grad_feats = jnp.sum(got.astype(jnp.float32), axis=0).T
    total_nodes = owned * row_count * col_count
    grad_weight = grad_weight / jnp.sqrt(jnp.float32(total_nodes))
    return (preact, grad_feats, grad_weight)


def solution(mesh):
    fine = Mesh(mesh.devices.reshape(tuple(SIZES.values())), tuple(SIZES))
    in_specs = (
        P(COL + ROW, None),
        P(),
        P(ROW, COL, None, None, None),
        P(ROW, COL, None),
        P(ROW, COL, None),
        P(ROW + COL, None),
        P(ROW + COL, None),
    )
    out_specs = (P(ROW + COL, None), P(COL + ROW, None), P())
    return jax.shard_map(shards, mesh=fine, in_specs=in_specs, out_specs=out_specs, check_vma=False)
```
